32 devices in a mesh: expert: 8 (over z, x), dp: 4 (over y, core).
Axes of the slice: x: 2, y: 2, z: 4, core: 2. Of those that a mesh axis runs over, the one named last changes fastest.
Arguments:
- tokens: bfloat16 [8, 240, 7168], P('expert', 'dp'), may hold values from -6 to 6
- cotangent: bfloat16 [8, 240, 7168], P('expert', 'dp'), may hold values from -1.5 to 1.5
- counts: int32 [8, 4], replicated, may hold values from 1 to 60, as said below
- w_gate: bfloat16 [8, 7168, 2048], P('expert', None, 'dp'), may hold values from -0.0625 to 0.0625
- w_up: bfloat16 [8, 7168, 2048], P('expert', None, 'dp'), may hold values from -0.0625 to 0.0625
- w_down: bfloat16 [8, 2048, 7168], P('expert', 'dp'), may hold values from -0.125 to 0.125
Outputs:
- outputs: bfloat16 [8, 240, 7168], P('expert', 'dp')
- input_grads: bfloat16 [8, 240, 7168], P('expert', 'dp')
- gate_grad: bfloat16 [8, 7168, 2048], P('expert', None, 'dp')
- up_grad: bfloat16 [8, 7168, 2048], P('expert', None, 'dp')
- down_grad: bfloat16 [8, 2048, 7168], P('expert', 'dp')
The draws below stay inside these ranges and needn't reach their ends.
Inputs may be any that keep to these rules, and one draw needn't show every extreme that they name: For each expert e below 4, exactly one of experts e and e + 4 is hot: all its counts exceed 40 - 20 and one equals 60; every count of the other is at most 20 and one equals 20.
All inputs are finite; a program needn't handle non-finite values.
Results may differ from the reference program's by a relative error of at most 0.012.
Values may be sent and summed in bfloat16 or wider, within the bound.
A program may use at most 192 MiB of HBM per device.

```python
import jax
import jax.numpy as jnp
from jax import lax

D = 7168
H = 2048
HOME = 40
SPILL = 20
CAP = 60
EXPERTS = 8
BATCHES = 4


def draw_counts(key, part):
    keys = jax.random.split(key, 5)
    half = EXPERTS // 2
    border = HOME - SPILL
    side = jax.random.randint(keys[0], (half, 1), 0, 2)
    hot_vals = jax.random.randint(keys[1], (half, BATCHES), border + 1, CAP + 1)
    cold_vals = jax.random.randint(keys[2], (half, BATCHES), 1, border + 1)
    batch_ids = jnp.arange(BATCHES)[None, :]
    hot_full = jax.random.randint(keys[3], (half, 1), 0, BATCHES)
    cold_full = jax.random.randint(keys[4], (half, 1), 0, BATCHES)
    hot_vals = jnp.where(batch_ids == hot_full, CAP, hot_vals)
    cold_vals = jnp.where(batch_ids == cold_full, border, cold_vals)
    lower = jnp.where(side == 0, hot_vals, cold_vals)
    upper = jnp.where(side == 0, cold_vals, hot_vals)
    return jnp.concatenate([lower, upper], axis=0).astype(jnp.int32)


def shard_levels(key, shape, cuts, low, high):
    def one(axis_at, blocks):
        draws = jax.random.uniform(jax.random.fold_in(jax.random.fold_in(key, 6), axis_at), (blocks,), jnp.float32, low / len(cuts), high / len(cuts))
        return jnp.repeat(jnp.exp(draws), shape[axis_at] // blocks).reshape((-1,) + (1,) * (len(shape) - axis_at - 1))

    factor_of = one(*cuts[0])
    for cut in cuts[1:]:
        factor_of = factor_of * one(*cut)
    return factor_of


def normal_values(key, extent, scale, reach, pieces=(), held_as=jnp.bfloat16):
    array = scale * jax.random.normal(key, extent, jnp.float32)
    if pieces:
        array = array * shard_levels(key, extent, pieces, -0.22, 0.18)
    return jnp.clip(array, -reach, reach).astype(held_as)


def setup_inputs(seed: int = 0) -> dict:
    splits = jax.random.split(jax.random.key(seed), 7)
    tokens = normal_values(splits[0], (EXPERTS, BATCHES * CAP, D), 1.0, 6.0, ((0, 8), (1, 4)))
    cotangent = normal_values(splits[1], (EXPERTS, BATCHES * CAP, D), 0.25, 1.5, ((0, 8), (1, 4)))
    counts = draw_counts(jax.random.fold_in(splits[6], 71), 0)
    w_gate = normal_values(splits[3], (EXPERTS, D, H), D ** -0.5, 0.0625, ((0, 8), (2, 4)))
    w_up = normal_values(splits[4], (EXPERTS, D, H), D ** -0.5, 0.0625, ((0, 8), (2, 4)))
    w_down = normal_values(splits[5], (EXPERTS, H, D), H ** -0.5, 0.125, ((0, 8), (1, 4)))
    return {"tokens": tokens, "cotangent": cotangent, "counts": counts, "w_gate": w_gate, "w_up": w_up, "w_down": w_down}


def silu_slope(value):
    sigma = jax.nn.sigmoid(value)
    return sigma * (1.0 + value * (1.0 - sigma))


def slice_total(parts):
    rounded = lax.optimization_barrier(parts.astype(jnp.bfloat16))
    return jnp.sum(rounded.astype(jnp.float32), axis=0).astype(jnp.bfloat16)


def one_expert(operands):
    rows_in, cot_in, count_row, gate_w, up_w, down_w = operands
    width = H // BATCHES
    valid = (jnp.arange(CAP, dtype=jnp.int32)[None, :] < count_row[:, None])[:, :, None]
    masked = jnp.where(valid, rows_in, jnp.zeros_like(rows_in))
    masked_cot = jnp.where(valid, cot_in, jnp.zeros_like(cot_in))
    flat = masked.reshape(BATCHES * CAP, D)
    flat_cot = masked_cot.reshape(BATCHES * CAP, D)
    gate = jnp.dot(flat, gate_w, preferred_element_type=jnp.float32)
    up = jnp.dot(flat, up_w, preferred_element_type=jnp.float32)
    active = jax.nn.silu(gate)
    hidden = (active * up).astype(jnp.bfloat16)
    out_parts = jnp.einsum("rbh,bhd->brd", hidden.reshape(-1, BATCHES, width).astype(jnp.float32),
                           down_w.reshape(BATCHES, width, D).astype(jnp.float32), precision=lax.Precision.HIGHEST)
    outputs = slice_total(out_parts)
    hidden_grad = jnp.dot(flat_cot, down_w.T, preferred_element_type=jnp.float32)
    gate_act = (hidden_grad * up * silu_slope(gate)).astype(jnp.bfloat16)
    up_act = (hidden_grad * active).astype(jnp.bfloat16)
    in_parts = jnp.einsum("rbh,dbh->brd", gate_act.reshape(-1, BATCHES, width).astype(jnp.float32),
                          gate_w.reshape(D, BATCHES, width).astype(jnp.float32), precision=lax.Precision.HIGHEST)
    in_parts = in_parts + jnp.einsum("rbh,dbh->brd", up_act.reshape(-1, BATCHES, width).astype(jnp.float32),
                                     up_w.reshape(D, BATCHES, width).astype(jnp.float32), precision=lax.Precision.HIGHEST)
    input_grads = slice_total(in_parts)

    def split_rows(values):
        shaped = values.reshape(BATCHES, CAP, values.shape[-1])
        return shaped[:, :HOME].reshape(-1, values.shape[-1]), shaped[:, HOME:].reshape(-1, values.shape[-1])

    rows_home, rows_spill = split_rows(flat)
    cot_home, cot_spill = split_rows(flat_cot)
    hid_home, hid_spill = split_rows(hidden)
    ga_home, ga_spill = split_rows(gate_act)
    ua_home, ua_spill = split_rows(up_act)

    def combine(home_term, spill_term):
        spill_round = lax.optimization_barrier(spill_term.astype(jnp.bfloat16))
        return (home_term + spill_round.astype(jnp.float32)).astype(jnp.bfloat16)

    gate_grad = combine(jnp.dot(rows_home.T, ga_home, preferred_element_type=jnp.float32),
                        jnp.dot(rows_spill.T, ga_spill, preferred_element_type=jnp.float32))
    up_grad = combine(jnp.dot(rows_home.T, ua_home, preferred_element_type=jnp.float32),
                      jnp.dot(rows_spill.T, ua_spill, preferred_element_type=jnp.float32))
    down_grad = combine(jnp.dot(hid_home.T, cot_home, preferred_element_type=jnp.float32),
                        jnp.dot(hid_spill.T, cot_spill, preferred_element_type=jnp.float32))
    return outputs, input_grads, gate_grad, up_grad, down_grad


def reference(tokens, cotangent, counts, w_gate, w_up, w_down):
    rows_all = tokens.reshape(EXPERTS, BATCHES, CAP, D)
    cot_all = cotangent.reshape(EXPERTS, BATCHES, CAP, D)
    outputs, input_grads, gate_grad, up_grad, down_grad = lax.map(
        one_expert, (rows_all, cot_all, counts, w_gate, w_up, w_down))
    return (outputs.reshape(EXPERTS, BATCHES * CAP, D), input_grads.reshape(EXPERTS, BATCHES * CAP, D),
            gate_grad, up_grad, down_grad)
```

```python
import jax
import jax.numpy as jnp
from jax import lax
from jax.sharding import PartitionSpec as P


def silu_slope(value):
    sigma = jax.nn.sigmoid(value)
    return sigma * (1.0 + value * (1.0 - sigma))


def contract_last(left, right):
    return lax.dot_general(
        left, right, (((1,), (1,)), ((), ())), preferred_element_type=jnp.float32
    )


def contract_first(left, right):
    return lax.dot_general(
        left, right, (((0,), (0,)), ((), ())), preferred_element_type=jnp.float32
    )


def shards(tokens, cotangent, counts, w_gate, w_up, w_down):
    gate_w = w_gate[0]
    up_w = w_up[0]
    down_w = w_down[0]
    own_total = counts[lax.axis_index("expert"), lax.axis_index("dp")]
    slots = tokens.shape[1]
    valid = (jnp.arange(slots, dtype=jnp.int32) < own_total)[:, None]
    both = jnp.stack([jnp.where(valid, tokens[0], 0), jnp.where(valid, cotangent[0], 0)])
    full = lax.all_gather(both, "dp", axis=1, tiled=True)
    rows, cot_rows = full[0], full[1]
    gate = jnp.dot(rows, gate_w, preferred_element_type=jnp.float32)
    up = jnp.dot(rows, up_w, preferred_element_type=jnp.float32)
    active = jax.nn.silu(gate)
    hidden = (active * up).astype(jnp.bfloat16)
    hidden_grad = contract_last(cot_rows, down_w)
    gate_act = (hidden_grad * up * silu_slope(gate)).astype(jnp.bfloat16)
    up_act = (hidden_grad * active).astype(jnp.bfloat16)
    out_part = jnp.dot(hidden, down_w, preferred_element_type=jnp.float32)
    in_part = contract_last(gate_act, gate_w) + contract_last(up_act, up_w)
    parts = jnp.stack([out_part.astype(jnp.bfloat16), in_part.astype(jnp.bfloat16)])
    sums = lax.psum_scatter(parts, "dp", scatter_dimension=1, tiled=True)
    gate_grad = contract_first(rows, gate_act).astype(jnp.bfloat16)
    up_grad = contract_first(rows, up_act).astype(jnp.bfloat16)
    down_grad = contract_first(hidden, cot_rows).astype(jnp.bfloat16)
    return (sums[0][None], sums[1][None], gate_grad[None], up_grad[None], down_grad[None])


def solution(mesh):
    by_row = P("expert", "dp", None)
    by_column = P("expert", None, "dp")
    return jax.shard_map(
        shards,
        mesh=mesh,
        in_specs=(by_row, by_row, P(), by_column, by_column, by_row),
        out_specs=(by_row, by_row, by_column, by_column, by_row),
        check_vma=False,
    )
```

```python
import functools

import jax
import jax.numpy as jnp
from jax import lax
from jax.experimental import pallas as pl
from jax.experimental.pallas import tpu as pltpu
from jax.sharding import PartitionSpec as P

MESH = pl.DeviceIdType.MESH
TILE = 1024
HALF = 32


def contract_last(left, right):
    return lax.dot_general(
        left, right, (((1,), (1,)), ((), ())), preferred_element_type=jnp.float32
    )


def contract_first(left, right):
    return lax.dot_general(
        left, right, (((0,), (0,)), ((), ())), preferred_element_type=jnp.float32
    )


def rows_kernel(chips, counts_ref, tok_ref, cot_ref, wg_hbm, wu_hbm, wd_hbm,
                xs_hbm, acts, own_hbm, back_hbm, ret_hbm,
                wg, wu, wd, x, acc, part_own, part, s_own, s_far,
                w_sem, sib_send, sib_recv, y_send, y_recv, f_send, f_recv,
                po_send, po_recv, ps_send, ps_recv, rt_send, rt_recv, l_sem):
    depth = tok_ref.shape[1]
    slots = tok_ref.shape[0]
    e = lax.axis_index("expert")
    p = lax.axis_index("dp")
    y = p // 2
    c = p % 2
    sibling = (e, y * 2 + 1 - c)

    def chip(step):
        return lax.rem(y + step, chips)

    def rows_at(chip_pos, half, core):
        return pl.ds(pl.multiple_of(((chip_pos * 2 + half) * 2 + core) * HALF, HALF), HALF)

    def columns(k):
        return pl.ds(pl.multiple_of(k * TILE, TILE), TILE)

    loads = [pltpu.make_async_copy(src, dst, w_sem.at[i])
             for i, (src, dst) in enumerate(((wg_hbm, wg), (wu_hbm, wu), (wd_hbm, wd)))]
    for load in loads:
        load.start()

    barrier = pltpu.get_barrier_semaphore()
    pl.semaphore_signal(barrier, inc=1, device_id=sibling, device_id_type=MESH)
    for step in range(1, chips):
        pl.semaphore_signal(barrier, inc=1, device_id=(e, chip(step) * 2 + c), device_id_type=MESH)

    count = counts_ref[e, p]
    first, second = rows_at(y, 0, c), rows_at(y, 1, c)
    tail = pl.ds(pl.multiple_of((y * 4 + 2 + c) * HALF, HALF), slots - HALF)

    @pl.loop(0, depth // TILE)
    def _(k):
        cols = columns(k)
        keep = lax.broadcasted_iota(jnp.int32, (slots, TILE), 0) < count
        for a, ref in enumerate((tok_ref, cot_ref)):
            value = jnp.where(keep, ref[:, cols].astype(jnp.float32), 0.0).astype(jnp.bfloat16)
            x[a, first, cols] = value[:HALF]
            x[a, second, cols] = jnp.zeros((HALF, TILE), jnp.bfloat16)
            x[a, tail, cols] = value[HALF:]

    pl.semaphore_wait(barrier, chips)

    def remote(src, dst, send, recv, device):
        return pltpu.make_async_remote_copy(
            src_ref=src, dst_ref=dst, send_sem=send, recv_sem=recv,
            device_id=device, device_id_type=MESH)

    def to_peer(step, half):
        block = x.at[:, rows_at(y, half, c), :]
        return remote(block, block, y_send.at[step - 1, half], y_recv.at[step - 1, half],
                      (e, chip(step) * 2 + c))

    def to_sibling(half):
        block = x.at[:, rows_at(y, half, c), :]
        return remote(block, block, sib_send.at[half], sib_recv.at[half], sibling)

    def forward(step, half):
        block = x.at[:, rows_at(chip(chips - step), half, c), :]
        return remote(block, block, f_send.at[step - 1, half], f_recv.at[step - 1, half], sibling)

    for half in range(2):
        for step in range(1, chips):
            to_peer(step, half).start()
    for half in range(2):
        to_sibling(half).start()

    def work(row0, count_rows, out):
        rows = pl.ds(pl.multiple_of(row0, 2 * HALF), count_rows)
        acc[:, :count_rows, :] = jnp.zeros((3, count_rows, acc.shape[2]), jnp.float32)

        @pl.loop(0, depth // TILE)
        def _(k):
            cols = columns(k)
            tok, cot = x[0, rows, cols], x[1, rows, cols]
            acc[0, :count_rows] += jnp.dot(tok, wg[cols, :], preferred_element_type=jnp.float32)
            acc[1, :count_rows] += jnp.dot(tok, wu[cols, :], preferred_element_type=jnp.float32)
            acc[2, :count_rows] += contract_last(cot, wd[:, cols])

        gate, up, hidden_grad = acc[0, :count_rows], acc[1, :count_rows], acc[2, :count_rows]
        sigma = jax.nn.sigmoid(gate)
        active = gate * sigma
        acts[0, rows] = (active * up).astype(jnp.bfloat16)
        acts[1, rows] = (hidden_grad * up * (sigma * (1.0 + gate * (1.0 - sigma)))).astype(jnp.bfloat16)
        acts[2, rows] = (hidden_grad * active).astype(jnp.bfloat16)

        @pl.loop(0, depth // TILE)
        def _(k):
            cols = columns(k)
            out[0, :, cols] = jnp.dot(
                acts[0, rows], wd[:, cols], preferred_element_type=jnp.float32).astype(jnp.bfloat16)
            out[1, :, cols] = (contract_last(acts[1, rows], wg[cols, :])
                               + contract_last(acts[2, rows], wu[cols, :])).astype(jnp.bfloat16)

    def add_into(total, term):
        @pl.loop(0, depth // TILE)
        def _(k):
            cols = columns(k)
            total[:, :, cols] = (total[:, :, cols].astype(jnp.float32)
                                 + term[:, :, cols].astype(jnp.float32)).astype(jnp.bfloat16)

    def core_rows(half, core):
        return pl.ds(pl.multiple_of((half * 2 + core) * HALF, HALF), HALF)

    for load in loads:
        load.wait()
    for half in range(2):
        to_sibling(half).wait_recv()
    work(y * 4 * HALF, 4 * HALF, part_own)

    def own_part(half):
        return remote(part_own.at[:, core_rows(half, 1 - c), :], s_own.at[half],
                      po_send.at[half], po_recv.at[half], sibling)

    for half in range(2):
        own_part(half).start()
    for half in range(2):
        own_part(half).wait_recv()
        add_into(s_own.at[half], part_own.at[:, core_rows(half, c), :])
    own_copy = pltpu.make_async_copy(s_own, own_hbm, l_sem.at[0])
    own_copy.start()

    def far_part(step, half, slot):
        return remote(part.at[slot, :, core_rows(0, 1 - c), :], s_far.at[step - 1, half],
                      ps_send.at[step - 1, half], ps_recv.at[step - 1, half], sibling)

    def give_back(step):
        return remote(s_far.at[step - 1, 0], back_hbm.at[step - 1], rt_send.at[step - 1],
                      rt_recv.at[step - 1], (e, chip(chips - step) * 2 + c))

    xs_copy = pltpu.make_async_copy(x, xs_hbm, l_sem.at[1])
    pending = [None, None]
    at = 0
    last = (1, chips - 1)
    for half in range(2):
        for step in range(1, chips):
            to_peer(step, half).wait_recv()
            forward(step, half).start()
            forward(step, half).wait_recv()
            if (half, step) == last:
                xs_copy.start()
            slot = at % 2
            at += 1
            if pending[slot] is not None:
                pending[slot].wait_send()
            work((chip(chips - step) * 2 + half) * 2 * HALF, 2 * HALF, part.at[slot])
            pending[slot] = far_part(step, half, slot)
            pending[slot].start()
            pending[slot].wait_recv()
            add_into(s_far.at[step - 1, half], part.at[slot, :, core_rows(0, c), :])
            if half == 0:
                give_back(step).start()
            else:
                pltpu.make_async_copy(s_far.at[step - 1, 1], ret_hbm.at[step - 1],
                                      l_sem.at[1 + step]).start()
    for transfer in pending:
        if transfer is not None:
            transfer.wait_send()
    for half in range(2):
        to_sibling(half).wait_send()
        own_part(half).wait_send()
        for step in range(1, chips):
            to_peer(step, half).wait_send()
            forward(step, half).wait_send()
    own_copy.wait()
    xs_copy.wait()
    for step in range(1, chips):
        pltpu.make_async_copy(s_far.at[step - 1, 1], ret_hbm.at[step - 1], l_sem.at[1 + step]).wait()
        give_back(step).wait()


def call_rows(chips, counts, tokens, cotangent, gate_w, up_w, down_w):
    depth, width = gate_w.shape
    rows = chips * 4 * HALF
    others = chips - 1
    dtype = jnp.bfloat16
    anywhere = pl.BlockSpec(memory_space=pl.ANY)
    vmem = pl.BlockSpec(memory_space=pltpu.VMEM)
    pairs = pltpu.SemaphoreType.DMA((others, 2))
    halves = pltpu.SemaphoreType.DMA((2,))
    return pl.pallas_call(
        functools.partial(rows_kernel, chips),
        out_shape=(
            jax.ShapeDtypeStruct((2, rows, depth), dtype),
            jax.ShapeDtypeStruct((3, rows, width), dtype),
            jax.ShapeDtypeStruct((2, 2, HALF, depth), dtype),
            jax.ShapeDtypeStruct((others, 2, HALF, depth), dtype),
            jax.ShapeDtypeStruct((others, 2, HALF, depth), dtype),
        ),
        in_specs=[pl.BlockSpec(memory_space=pltpu.SMEM), vmem, vmem, anywhere, anywhere, anywhere],
        out_specs=(anywhere, vmem, anywhere, anywhere, anywhere),
        scratch_shapes=[
            pltpu.VMEM((depth, width), dtype),
            pltpu.VMEM((depth, width), dtype),
            pltpu.VMEM((width, depth), dtype),
            pltpu.VMEM((2, rows, depth), dtype),
            pltpu.VMEM((3, 4 * HALF, width), jnp.float32),
            pltpu.VMEM((2, 4 * HALF, depth), dtype),
            pltpu.VMEM((2, 2, 2 * HALF, depth), dtype),
            pltpu.VMEM((2, 2, HALF, depth), dtype),
            pltpu.VMEM((others, 2, 2, HALF, depth), dtype),
            pltpu.SemaphoreType.DMA((3,)),
            halves, halves, pairs, pairs, pairs, pairs, halves, halves, pairs, pairs,
            pltpu.SemaphoreType.DMA((others,)),
            pltpu.SemaphoreType.DMA((others,)),
            pltpu.SemaphoreType.DMA((2 + others,)),
        ],
        compiler_params=pltpu.CompilerParams(
            collective_id=0, has_side_effects=True, vmem_limit_bytes=60 * 1024 * 1024),
    )(counts, tokens, cotangent, gate_w, up_w, down_w)


def shards(chips, tokens, cotangent, counts, w_gate, w_up, w_down):
    slots = tokens.shape[1]
    xs, acts, own, back, ret = call_rows(
        chips, counts, tokens[0], cotangent[0], w_gate[0], w_up[0], w_down[0])
    got = []
    for step in range(1, chips):
        pairs = [(q * 2 + c, (q - step) % chips * 2 + c) for q in range(chips) for c in range(2)]
        got.append(lax.ppermute(ret[step - 1], "dp", pairs))
    gate_grad = contract_first(xs[0], acts[1]).astype(jnp.bfloat16)
    up_grad = contract_first(xs[0], acts[2]).astype(jnp.bfloat16)
    down_grad = contract_first(acts[0], xs[1]).astype(jnp.bfloat16)
    firsts, seconds = own[0].astype(jnp.float32), own[1].astype(jnp.float32)
    for step in range(1, chips):
        firsts = firsts + back[step - 1].astype(jnp.float32)
        seconds = seconds + got[step - 1].astype(jnp.float32)
    sums = [
        jnp.concatenate([firsts[a], seconds[a, :slots - HALF]], axis=0).astype(jnp.bfloat16)
        for a in range(2)
    ]
    return (sums[0][None], sums[1][None], gate_grad[None], up_grad[None], down_grad[None])


def solution(mesh):
    by_row = P("expert", "dp", None)
    by_column = P("expert", None, "dp")
    return jax.shard_map(
        functools.partial(shards, mesh.shape["dp"] // 2),
        mesh=mesh,
        in_specs=(by_row, by_row, P(), by_column, by_column, by_row),
        out_specs=(by_row, by_row, by_column, by_column, by_row),
        check_vma=False,
    )
```

```python
import functools

import jax
import jax.numpy as jnp
from jax import lax
from jax.experimental import pallas as pl
from jax.experimental.pallas import tpu as pltpu
from jax.sharding import PartitionSpec as P

MESH = pl.DeviceIdType.MESH
TILE = 1024
HALF = 32
SIDE = 512


def contract_last(left, right):
    return lax.dot_general(
        left, right, (((1,), (1,)), ((), ())), preferred_element_type=jnp.float32
    )


def contract_first(left, right):
    return lax.dot_general(
        left, right, (((0,), (0,)), ((), ())), preferred_element_type=jnp.float32
    )


def rows_kernel(chips, counts_ref, tok_ref, cot_ref, wg_hbm, wu_hbm, wd_hbm,
                xs_hbm, acts, own_hbm, back_hbm, ret_hbm,
                wg, wu, wd, x, acc, part_own, part, s_own, s_far, pk, pk_got, rp, rp_got,
                w_sem, sib_send, sib_recv, y_send, y_recv, f_send, f_recv,
                po_send, po_recv, ps_send, ps_recv, rt_send, rt_recv, k_send, k_recv, l_sem):
    depth = tok_ref.shape[1]
    slots = tok_ref.shape[0]
    e = lax.axis_index("expert")
    p = lax.axis_index("dp")
    y = p // 2
    c = p % 2
    sibling = (e, y * 2 + 1 - c)

    def chip(step):
        return lax.rem(y + step, chips)

    def rows_at(chip_pos, half, core):
        return pl.ds(pl.multiple_of(((chip_pos * 2 + half) * 2 + core) * HALF, HALF), HALF)

    def columns(k):
        return pl.ds(pl.multiple_of(k * TILE, TILE), TILE)

    loads = [pltpu.make_async_copy(src, dst, w_sem.at[i])
             for i, (src, dst) in enumerate(((wg_hbm, wg), (wu_hbm, wu), (wd_hbm, wd)))]
    for load in loads:
        load.start()

    barrier = pltpu.get_barrier_semaphore()
    pl.semaphore_signal(barrier, inc=1, device_id=sibling, device_id_type=MESH)
    for step in range(1, chips):
        pl.semaphore_signal(barrier, inc=1, device_id=(e, chip(step) * 2 + c), device_id_type=MESH)

    table = counts_ref[...]
    here = jnp.logical_and(lax.broadcasted_iota(jnp.int32, table.shape, 0) == e,
                           lax.broadcasted_iota(jnp.int32, table.shape, 1) == p)
    picked = jnp.where(here, table.astype(jnp.float32), 0.0)
    count = jnp.sum(jnp.sum(picked, axis=1, keepdims=True), axis=0, keepdims=True)

    def mask_half(half):
        filled = min(HALF, slots - half * HALF)
        start = ((y * 2 + half) * 2 + c) * HALF
        rows = pl.ds(pl.multiple_of(start, HALF), filled)

        @pl.loop(0, depth // TILE)
        def _(k):
            cols = columns(k)
            slot = (lax.broadcasted_iota(jnp.int32, (filled, TILE), 0) + half * HALF).astype(jnp.float32)
            keep = slot < count
            for a, ref in enumerate((tok_ref, cot_ref)):
                value = ref[half * HALF:half * HALF + filled, cols].astype(jnp.float32)
                if filled < HALF:
                    x[a, rows_at(y, half, c), cols] = jnp.zeros((HALF, TILE), jnp.bfloat16)
                x[a, rows, cols] = jnp.where(keep, value, 0.0).astype(jnp.bfloat16)

    extra = slots - HALF - 16
    middle = depth // 2

    def selection(side, transposed):
        shape = (32, 4 * extra) if transposed else (4 * extra, 32)
        packed = lax.broadcasted_iota(jnp.int32, shape, 1 if transposed else 0)
        row = lax.broadcasted_iota(jnp.int32, shape, 0 if transposed else 1)
        hit = None
        for a in range(2):
            start = (2 * a + side) * extra
            inside = jnp.logical_and(packed >= start, packed < start + extra)
            match = jnp.logical_and(inside, packed - start == row - 16 * a)
            hit = match if hit is None else jnp.logical_or(hit, match)
        return jnp.where(hit, 1.0, 0.0).astype(jnp.bfloat16)

    def side_columns(side, k):
        return pl.ds(pl.multiple_of(side * middle + k * SIDE, SIDE), SIDE)

    def pack(src, rows, dst):
        picks = [selection(side, False) for side in range(2)]

        @pl.loop(0, middle // SIDE)
        def _(k):
            total = None
            for side in range(2):
                cols = side_columns(side, k)
                both = jnp.concatenate([src[0, rows, cols], src[1, rows, cols]], axis=0)
                term = jnp.dot(picks[side], both, preferred_element_type=jnp.float32)
                total = term if total is None else total + term
            dst[:, side_columns(0, k)] = total.astype(jnp.bfloat16)

    def unpack(src, dst, rows):
        picks = [selection(side, True) for side in range(2)]

        @pl.loop(0, middle // SIDE)
        def _(k):
            value = src[:, side_columns(0, k)]
            for side in range(2):
                cols = side_columns(side, k)
                both = jnp.dot(picks[side], value, preferred_element_type=jnp.float32).astype(jnp.bfloat16)
                dst[0, rows, cols] = both[:16]
                dst[1, rows, cols] = both[16:]

    def sixteen(chip_pos, core, part_of):
        start = ((chip_pos * 2 + 1) * 2 + core) * HALF + part_of * 16
        return pl.ds(pl.multiple_of(start, 16), 16)

    def remote(src, dst, send, recv, device):
        return pltpu.make_async_remote_copy(
            src_ref=src, dst_ref=dst, send_sem=send, recv_sem=recv,
            device_id=device, device_id_type=MESH)

    def to_peer(step, half):
        block = x.at[:, sixteen(y, c, 0) if half else rows_at(y, half, c), :]
        return remote(block, block, y_send.at[step - 1, half], y_recv.at[step - 1, half],
                      (e, chip(step) * 2 + c))

    def tail_to_peer(step):
        return remote(pk, pk_got.at[step - 1], k_send.at[step - 1, 0], k_recv.at[step - 1, 0],
                      (e, chip(step) * 2 + c))

    def to_sibling(half):
        block = x.at[:, rows_at(y, half, c), :]
        return remote(block, block, sib_send.at[half], sib_recv.at[half], sibling)

    def forward(step, half):
        block = x.at[:, rows_at(chip(chips - step), half, c), :]
        return remote(block, block, f_send.at[step - 1, half], f_recv.at[step - 1, half], sibling)

    mask_half(1)
    pl.semaphore_wait(barrier, chips)
    for step in range(1, chips):
        to_peer(step, 1).start()
    pack(x, sixteen(y, c, 1), pk)
    for step in range(1, chips):
        tail_to_peer(step).start()
    mask_half(0)
    for step in range(1, chips):
        to_peer(step, 0).start()
    for half in range(2):
        to_sibling(half).start()

    def work(row0, count_rows, out):
        rows = pl.ds(pl.multiple_of(row0, 2 * HALF), count_rows)
        acc[:, :count_rows, :] = jnp.zeros((3, count_rows, acc.shape[2]), jnp.float32)

        @pl.loop(0, depth // TILE)
        def _(k):
            cols = columns(k)
            tok, cot = x[0, rows, cols], x[1, rows, cols]
            acc[0, :count_rows] += jnp.dot(tok, wg[cols, :], preferred_element_type=jnp.float32)
            acc[1, :count_rows] += jnp.dot(tok, wu[cols, :], preferred_element_type=jnp.float32)
            acc[2, :count_rows] += contract_last(cot, wd[:, cols])

        gate, up, hidden_grad = acc[0, :count_rows], acc[1, :count_rows], acc[2, :count_rows]
        sigma = jax.nn.sigmoid(gate)
        active = gate * sigma
        acts[0, rows] = (active * up).astype(jnp.bfloat16)
        acts[1, rows] = (hidden_grad * up * (sigma * (1.0 + gate * (1.0 - sigma)))).astype(jnp.bfloat16)
        acts[2, rows] = (hidden_grad * active).astype(jnp.bfloat16)

        @pl.loop(0, depth // TILE)
        def _(k):
            cols = columns(k)
            out[0, :, cols] = jnp.dot(
                acts[0, rows], wd[:, cols], preferred_element_type=jnp.float32).astype(jnp.bfloat16)
            out[1, :, cols] = (contract_last(acts[1, rows], wg[cols, :])
                               + contract_last(acts[2, rows], wu[cols, :])).astype(jnp.bfloat16)

    def add_into(total, term):
        @pl.loop(0, depth // TILE)
        def _(k):
            cols = columns(k)
            total[:, :, cols] = (total[:, :, cols].astype(jnp.float32)
                                 + term[:, :, cols].astype(jnp.float32)).astype(jnp.bfloat16)

    def core_rows(half, core):
        return pl.ds(pl.multiple_of((half * 2 + core) * HALF, HALF), HALF)

    for load in loads:
        load.wait()
    for half in range(2):
        to_sibling(half).wait_recv()
    work(y * 4 * HALF, 4 * HALF, part_own)

    def own_part(half):
        return remote(part_own.at[:, core_rows(half, 1 - c), :], s_own.at[half],
                      po_send.at[half], po_recv.at[half], sibling)

    for half in range(2):
        own_part(half).start()
    for half in range(2):
        own_part(half).wait_recv()
        add_into(s_own.at[half], part_own.at[:, core_rows(half, c), :])
    own_copy = pltpu.make_async_copy(s_own, own_hbm, l_sem.at[0])
    own_copy.start()

    def far_part(step, half, slot):
        return remote(part.at[slot, :, core_rows(0, 1 - c), :], s_far.at[step - 1, half],
                      ps_send.at[step - 1, half], ps_recv.at[step - 1, half], sibling)

    def give_back(step):
        return remote(s_far.at[step - 1, 1, :, 0:16, :], back_hbm.at[step - 1, :, 0:16, :],
                      rt_send.at[step - 1], rt_recv.at[step - 1], (e, chip(chips - step) * 2 + c))

    def tail_back(step):
        return remote(rp.at[step - 1], rp_got.at[step - 1], k_send.at[step - 1, 1], k_recv.at[step - 1, 1],
                      (e, chip(chips - step) * 2 + c))

    def back_copy(step):
        return pltpu.make_async_copy(s_far.at[step - 1, 1, :, 16:32, :],
                                     back_hbm.at[step - 1, :, 16:32, :], l_sem.at[1 + chips + step - 1])

    def ret_copy(step):
        return pltpu.make_async_copy(s_far.at[step - 1, 0], ret_hbm.at[step - 1], l_sem.at[1 + step])

    xs_copy = pltpu.make_async_copy(x, xs_hbm, l_sem.at[1])
    pending = [None, None]
    at = 0
    last = (0, chips - 1)
    for half in (1, 0):
        for step in range(1, chips):
            to_peer(step, half).wait_recv()
            if half:
                tail_to_peer(step).wait_recv()
                unpack(pk_got.at[step - 1], x, sixteen(chip(chips - step), c, 1))
            forward(step, half).start()
            forward(step, half).wait_recv()
            if (half, step) == last:
                xs_copy.start()
            slot = at % 2
            at += 1
            if pending[slot] is not None:
                pending[slot].wait_send()
            work((chip(chips - step) * 2 + half) * 2 * HALF, 2 * HALF, part.at[slot])
            pending[slot] = far_part(step, half, slot)
            pending[slot].start()
            pending[slot].wait_recv()
            add_into(s_far.at[step - 1, half], part.at[slot, :, core_rows(0, c), :])
            if half:
                give_back(step).start()
                pack(s_far.at[step - 1, 1], pl.ds(16, 16), rp.at[step - 1])
                tail_back(step).start()
            else:
                ret_copy(step).start()
    for transfer in pending:
        if transfer is not None:
            transfer.wait_send()
    for half in range(2):
        to_sibling(half).wait_send()
        own_part(half).wait_send()
        for step in range(1, chips):
            to_peer(step, half).wait_send()
            forward(step, half).wait_send()
    own_copy.wait()
    xs_copy.wait()
    for step in range(1, chips):
        tail_to_peer(step).wait_send()
        ret_copy(step).wait()
        give_back(step).wait()
        tail_back(step).wait()
        unpack(rp_got.at[step - 1], s_far.at[step - 1, 1], pl.ds(16, 16))
        back_copy(step).start()
    for step in range(1, chips):
        back_copy(step).wait()


def call_rows(chips, counts, tokens, cotangent, gate_w, up_w, down_w):
    depth, width = gate_w.shape
    rows = chips * 4 * HALF
    others = chips - 1
    tail = (4 * (tokens.shape[0] - HALF - 16), depth // 2)
    dtype = jnp.bfloat16
    anywhere = pl.BlockSpec(memory_space=pl.ANY)
    vmem = pl.BlockSpec(memory_space=pltpu.VMEM)
    pairs = pltpu.SemaphoreType.DMA((others, 2))
    halves = pltpu.SemaphoreType.DMA((2,))
    return pl.pallas_call(
        functools.partial(rows_kernel, chips),
        out_shape=(
            jax.ShapeDtypeStruct((2, rows, depth), dtype),
            jax.ShapeDtypeStruct((3, rows, width), dtype),
            jax.ShapeDtypeStruct((2, 2, HALF, depth), dtype),
            jax.ShapeDtypeStruct((others, 2, HALF, depth), dtype),
            jax.ShapeDtypeStruct((others, 2, HALF, depth), dtype),
        ),
        in_specs=[vmem, vmem, vmem, anywhere, anywhere, anywhere],
        out_specs=(anywhere, vmem, anywhere, anywhere, anywhere),
        scratch_shapes=[
            pltpu.VMEM((depth, width), dtype),
            pltpu.VMEM((depth, width), dtype),
            pltpu.VMEM((width, depth), dtype),
            pltpu.VMEM((2, rows, depth), dtype),
            pltpu.VMEM((3, 4 * HALF, width), jnp.float32),
            pltpu.VMEM((2, 4 * HALF, depth), dtype),
            pltpu.VMEM((2, 2, 2 * HALF, depth), dtype),
            pltpu.VMEM((2, 2, HALF, depth), dtype),
            pltpu.VMEM((others, 2, 2, HALF, depth), dtype),
            pltpu.VMEM(tail, dtype),
            pltpu.VMEM((others,) + tail, dtype),
            pltpu.VMEM((others,) + tail, dtype),
            pltpu.VMEM((others,) + tail, dtype),
            pltpu.SemaphoreType.DMA((3,)),
            halves, halves, pairs, pairs, pairs, pairs, halves, halves, pairs, pairs,
            pltpu.SemaphoreType.DMA((others,)),
            pltpu.SemaphoreType.DMA((others,)),
            pairs, pairs,
            pltpu.SemaphoreType.DMA((2 + 2 * others,)),
        ],
        compiler_params=pltpu.CompilerParams(
            collective_id=0, has_side_effects=True, vmem_limit_bytes=60 * 1024 * 1024),
    )(counts, tokens, cotangent, gate_w, up_w, down_w)


def shards(chips, tokens, cotangent, counts, w_gate, w_up, w_down):
    slots = tokens.shape[1]
    xs, acts, own, back, ret = call_rows(
        chips, counts, tokens[0], cotangent[0], w_gate[0], w_up[0], w_down[0])
    got = []
    for step in range(1, chips):
        pairs = [(q * 2 + c, (q - step) % chips * 2 + c) for q in range(chips) for c in range(2)]
        got.append(lax.ppermute(ret[step - 1], "dp", pairs))
    gate_grad = contract_first(xs[0], acts[1]).astype(jnp.bfloat16)
    up_grad = contract_first(xs[0], acts[2]).astype(jnp.bfloat16)
    down_grad = contract_first(acts[0], xs[1]).astype(jnp.bfloat16)
    firsts, seconds = own[0].astype(jnp.float32), own[1].astype(jnp.float32)
    for step in range(1, chips):
        firsts = firsts + got[step - 1].astype(jnp.float32)
        seconds = seconds + back[step - 1].astype(jnp.float32)
    sums = [
        jnp.concatenate([firsts[a], seconds[a, :slots - HALF]], axis=0).astype(jnp.bfloat16)
        for a in range(2)
    ]
    return (sums[0][None], sums[1][None], gate_grad[None], up_grad[None], down_grad[None])


def solution(mesh):
    by_row = P("expert", "dp", None)
    by_column = P("expert", None, "dp")
    return jax.shard_map(
        functools.partial(shards, mesh.shape["dp"] // 2),
        mesh=mesh,
        in_specs=(by_row, by_row, P(), by_column, by_column, by_row),
        out_specs=(by_row, by_row, by_column, by_column, by_row),
        check_vma=False,
    )
```

```python
import functools

import jax
import jax.numpy as jnp
from jax import lax
from jax.experimental import pallas as pl
from jax.experimental.pallas import tpu as pltpu
from jax.sharding import PartitionSpec as P

MESH = pl.DeviceIdType.MESH
TILE = 1024
HALF = 32
SIDE = 512


def contract_last(left, right):
    return lax.dot_general(
        left, right, (((1,), (1,)), ((), ())), preferred_element_type=jnp.float32
    )


def contract_first(left, right):
    return lax.dot_general(
        left, right, (((0,), (0,)), ((), ())), preferred_element_type=jnp.float32
    )


def rows_kernel(chips, counts_ref, tok_ref, cot_ref, wg_hbm, wu_hbm, wd_hbm,
                xs_hbm, acts, own_hbm, back_hbm, ret_hbm,
                wg, wu, wd, x, acc, part_own, part, s_own, s_far, pk, pk_got, rp, rp_got,
                w_sem, sib_send, sib_recv, y_send, y_recv, f_send, f_recv,
                po_send, po_recv, ps_send, ps_recv, rt_send, rt_recv, k_send, k_recv, l_sem):
    depth = tok_ref.shape[1]
    slots = tok_ref.shape[0]
    e = lax.axis_index("expert")
    p = lax.axis_index("dp")
    y = p // 2
    c = p % 2
    sibling = (e, y * 2 + 1 - c)

    def chip(step):
        return lax.rem(y + step, chips)

    def rows_at(chip_pos, half, core):
        return pl.ds(pl.multiple_of(((chip_pos * 2 + half) * 2 + core) * HALF, HALF), HALF)

    def columns(k):
        return pl.ds(pl.multiple_of(k * TILE, TILE), TILE)

    loads = [pltpu.make_async_copy(src, dst, w_sem.at[i])
             for i, (src, dst) in enumerate(((wg_hbm, wg), (wu_hbm, wu), (wd_hbm, wd)))]
    for load in loads:
        load.start()

    barrier = pltpu.get_barrier_semaphore()
    pl.semaphore_signal(barrier, inc=1, device_id=sibling, device_id_type=MESH)
    for step in range(1, chips):
        pl.semaphore_signal(barrier, inc=1, device_id=(e, chip(step) * 2 + c), device_id_type=MESH)

    table = counts_ref[...]
    here = jnp.logical_and(lax.broadcasted_iota(jnp.int32, table.shape, 0) == e,
                           lax.broadcasted_iota(jnp.int32, table.shape, 1) == p)
    picked = jnp.where(here, table.astype(jnp.float32), 0.0)
    count = jnp.sum(jnp.sum(picked, axis=1, keepdims=True), axis=0, keepdims=True)

    def mask_half(half):
        filled = min(HALF, slots - half * HALF)
        start = ((y * 2 + half) * 2 + c) * HALF
        rows = pl.ds(pl.multiple_of(start, HALF), filled)

        @pl.loop(0, depth // TILE)
        def _(k):
            cols = columns(k)
            slot = (lax.broadcasted_iota(jnp.int32, (filled, TILE), 0) + half * HALF).astype(jnp.float32)
            keep = slot < count
            for a, ref in enumerate((tok_ref, cot_ref)):
                value = ref[half * HALF:half * HALF + filled, cols].astype(jnp.float32)
                if filled < HALF:
                    x[a, rows_at(y, half, c), cols] = jnp.zeros((HALF, TILE), jnp.bfloat16)
                x[a, rows, cols] = jnp.where(keep, value, 0.0).astype(jnp.bfloat16)

    extra = slots - HALF - 16
    middle = depth // 2

    def selection(side, transposed):
        shape = (32, 4 * extra) if transposed else (4 * extra, 32)
        packed = lax.broadcasted_iota(jnp.int32, shape, 1 if transposed else 0)
        row = lax.broadcasted_iota(jnp.int32, shape, 0 if transposed else 1)
        hit = None
        for a in range(2):
            start = (2 * a + side) * extra
            inside = jnp.logical_and(packed >= start, packed < start + extra)
            match = jnp.logical_and(inside, packed - start == row - 16 * a)
            hit = match if hit is None else jnp.logical_or(hit, match)
        return jnp.where(hit, 1.0, 0.0).astype(jnp.bfloat16)

    def side_columns(side, k):
        return pl.ds(pl.multiple_of(side * middle + k * SIDE, SIDE), SIDE)

    def pack(src, rows, dst):
        picks = [selection(side, False) for side in range(2)]

        @pl.loop(0, middle // SIDE)
        def _(k):
            total = None
            for side in range(2):
                cols = side_columns(side, k)
                both = jnp.concatenate([src[0, rows, cols], src[1, rows, cols]], axis=0)
                term = jnp.dot(picks[side], both, preferred_element_type=jnp.float32)
                total = term if total is None else total + term
            dst[:, side_columns(0, k)] = total.astype(jnp.bfloat16)

    def unpack(src, dst, rows):
        picks = [selection(side, True) for side in range(2)]

        @pl.loop(0, middle // SIDE)
        def _(k):
            value = src[:, side_columns(0, k)]
            for side in range(2):
                cols = side_columns(side, k)
                both = jnp.dot(picks[side], value, preferred_element_type=jnp.float32).astype(jnp.bfloat16)
                dst[0, rows, cols] = both[:16]
                dst[1, rows, cols] = both[16:]

    def sixteen(chip_pos, core, part_of):
        start = ((chip_pos * 2 + 1) * 2 + core) * HALF + part_of * 16
        return pl.ds(pl.multiple_of(start, 16), 16)

    def remote(src, dst, send, recv, device):
        return pltpu.make_async_remote_copy(
            src_ref=src, dst_ref=dst, send_sem=send, recv_sem=recv,
            device_id=device, device_id_type=MESH)

    def to_peer(step, half):
        block = x.at[:, sixteen(y, c, 0) if half else rows_at(y, half, c), :]
        return remote(block, block, y_send.at[step - 1, half], y_recv.at[step - 1, half],
                      (e, chip(step) * 2 + c))

    def tail_to_peer(step):
        return remote(pk, pk_got.at[step - 1], k_send.at[step - 1, 0], k_recv.at[step - 1, 0],
                      (e, chip(step) * 2 + c))

    def to_sibling(half):
        block = x.at[:, rows_at(y, half, c), :]
        return remote(block, block, sib_send.at[half], sib_recv.at[half], sibling)

    def forward(step, half):
        block = x.at[:, rows_at(chip(chips - step), half, c), :]
        return remote(block, block, f_send.at[step - 1, half], f_recv.at[step - 1, half], sibling)

    mask_half(1)
    pl.semaphore_wait(barrier, chips)
    for step in range(1, chips):
        to_peer(step, 1).start()
    pack(x, sixteen(y, c, 1), pk)
    for step in range(1, chips):
        tail_to_peer(step).start()
    mask_half(0)
    for step in range(1, chips):
        to_peer(step, 0).start()
    for half in range(2):
        to_sibling(half).start()

    def work(row0, count_rows, out):
        rows = pl.ds(pl.multiple_of(row0, 2 * HALF), count_rows)
        acc[:, :count_rows, :] = jnp.zeros((3, count_rows, acc.shape[2]), jnp.float32)

        @pl.loop(0, depth // TILE)
        def _(k):
            cols = columns(k)
            tok, cot = x[0, rows, cols], x[1, rows, cols]
            acc[0, :count_rows] += jnp.dot(tok, wg[cols, :], preferred_element_type=jnp.float32)
            acc[1, :count_rows] += jnp.dot(tok, wu[cols, :], preferred_element_type=jnp.float32)
            acc[2, :count_rows] += contract_last(cot, wd[:, cols])

        gate, up, hidden_grad = acc[0, :count_rows], acc[1, :count_rows], acc[2, :count_rows]
        sigma = jax.nn.sigmoid(gate)
        active = gate * sigma
        acts[0, rows] = (active * up).astype(jnp.bfloat16)
        acts[1, rows] = (hidden_grad * up * (sigma * (1.0 + gate * (1.0 - sigma)))).astype(jnp.bfloat16)
        acts[2, rows] = (hidden_grad * active).astype(jnp.bfloat16)

        @pl.loop(0, depth // TILE)
        def _(k):
            cols = columns(k)
            out[0, :, cols] = jnp.dot(
                acts[0, rows], wd[:, cols], preferred_element_type=jnp.float32).astype(jnp.bfloat16)
            out[1, :, cols] = (contract_last(acts[1, rows], wg[cols, :])
                               + contract_last(acts[2, rows], wu[cols, :])).astype(jnp.bfloat16)

    def add_into(total, term):
        @pl.loop(0, depth // TILE)
        def _(k):
            cols = columns(k)
            total[:, :, cols] = (total[:, :, cols].astype(jnp.float32)
                                 + term[:, :, cols].astype(jnp.float32)).astype(jnp.bfloat16)

    def core_rows(half, core):
        return pl.ds(pl.multiple_of((half * 2 + core) * HALF, HALF), HALF)

    for load in loads:
        load.wait()
    for half in range(2):
        to_sibling(half).wait_recv()
    work(y * 4 * HALF, 4 * HALF, part_own)

    def own_part(half):
        return remote(part_own.at[:, core_rows(half, 1 - c), :], s_own.at[half],
                      po_send.at[half], po_recv.at[half], sibling)

    for half in range(2):
        own_part(half).start()

    def far_part(step, half, slot):
        return remote(part.at[slot, :, core_rows(0, 1 - c), :], s_far.at[step - 1, half],
                      ps_send.at[step - 1, half], ps_recv.at[step - 1, half], sibling)

    def give_back(step):
        return remote(s_far.at[step - 1, 1, :, 0:16, :], back_hbm.at[step - 1, :, 0:16, :],
                      rt_send.at[step - 1], rt_recv.at[step - 1], (e, chip(chips - step) * 2 + c))

    def tail_back(step):
        return remote(rp.at[step - 1], rp_got.at[step - 1], k_send.at[step - 1, 1], k_recv.at[step - 1, 1],
                      (e, chip(chips - step) * 2 + c))

    def back_copy(step):
        return pltpu.make_async_copy(s_far.at[step - 1, 1, :, 16:32, :],
                                     back_hbm.at[step - 1, :, 16:32, :], l_sem.at[1 + chips + step - 1])

    def ret_copy(step):
        return pltpu.make_async_copy(s_far.at[step - 1, 0], ret_hbm.at[step - 1], l_sem.at[1 + step])

    xs_copy = pltpu.make_async_copy(x, xs_hbm, l_sem.at[1])
    pending = [None, None]
    at = 0
    last = (0, chips - 1)
    for half in (1, 0):
        for step in range(1, chips):
            to_peer(step, half).wait_recv()
            if half:
                tail_to_peer(step).wait_recv()
                unpack(pk_got.at[step - 1], x, sixteen(chip(chips - step), c, 1))
            forward(step, half).start()
            forward(step, half).wait_recv()
            if (half, step) == last:
                xs_copy.start()
            slot = at % 2
            at += 1
            if pending[slot] is not None:
                pending[slot].wait_send()
            work((chip(chips - step) * 2 + half) * 2 * HALF, 2 * HALF, part.at[slot])
            pending[slot] = far_part(step, half, slot)
            pending[slot].start()
            pending[slot].wait_recv()
            add_into(s_far.at[step - 1, half], part.at[slot, :, core_rows(0, c), :])
            if half:
                give_back(step).start()
                pack(s_far.at[step - 1, 1], pl.ds(16, 16), rp.at[step - 1])
                tail_back(step).start()
            else:
                ret_copy(step).start()
    for half in range(2):
        own_part(half).wait_recv()
        add_into(s_own.at[half], part_own.at[:, core_rows(half, c), :])
    own_copy = pltpu.make_async_copy(s_own, own_hbm, l_sem.at[0])
    own_copy.start()
    for transfer in pending:
        if transfer is not None:
            transfer.wait_send()
    for half in range(2):
        to_sibling(half).wait_send()
        own_part(half).wait_send()
        for step in range(1, chips):
            to_peer(step, half).wait_send()
            forward(step, half).wait_send()
    own_copy.wait()
    xs_copy.wait()
    for step in range(1, chips):
        tail_to_peer(step).wait_send()
        ret_copy(step).wait()
        give_back(step).wait()
        tail_back(step).wait()
        unpack(rp_got.at[step - 1], s_far.at[step - 1, 1], pl.ds(16, 16))
        back_copy(step).start()
    for step in range(1, chips):
        back_copy(step).wait()


def call_rows(chips, counts, tokens, cotangent, gate_w, up_w, down_w):
    depth, width = gate_w.shape
    rows = chips * 4 * HALF
    others = chips - 1
    tail = (4 * (tokens.shape[0] - HALF - 16), depth // 2)
    dtype = jnp.bfloat16
    anywhere = pl.BlockSpec(memory_space=pl.ANY)
    vmem = pl.BlockSpec(memory_space=pltpu.VMEM)
    pairs = pltpu.SemaphoreType.DMA((others, 2))
    halves = pltpu.SemaphoreType.DMA((2,))
    return pl.pallas_call(
        functools.partial(rows_kernel, chips),
        out_shape=(
            jax.ShapeDtypeStruct((2, rows, depth), dtype),
            jax.ShapeDtypeStruct((3, rows, width), dtype),
            jax.ShapeDtypeStruct((2, 2, HALF, depth), dtype),
            jax.ShapeDtypeStruct((others, 2, HALF, depth), dtype),
            jax.ShapeDtypeStruct((others, 2, HALF, depth), dtype),
        ),
        in_specs=[vmem, vmem, vmem, anywhere, anywhere, anywhere],
        out_specs=(anywhere, vmem, anywhere, anywhere, anywhere),
        scratch_shapes=[
            pltpu.VMEM((depth, width), dtype),
            pltpu.VMEM((depth, width), dtype),
            pltpu.VMEM((width, depth), dtype),
            pltpu.VMEM((2, rows, depth), dtype),
            pltpu.VMEM((3, 4 * HALF, width), jnp.float32),
            pltpu.VMEM((2, 4 * HALF, depth), dtype),
            pltpu.VMEM((2, 2, 2 * HALF, depth), dtype),
            pltpu.VMEM((2, 2, HALF, depth), dtype),
            pltpu.VMEM((others, 2, 2, HALF, depth), dtype),
            pltpu.VMEM(tail, dtype),
            pltpu.VMEM((others,) + tail, dtype),
            pltpu.VMEM((others,) + tail, dtype),
            pltpu.VMEM((others,) + tail, dtype),
            pltpu.SemaphoreType.DMA((3,)),
            halves, halves, pairs, pairs, pairs, pairs, halves, halves, pairs, pairs,
            pltpu.SemaphoreType.DMA((others,)),
            pltpu.SemaphoreType.DMA((others,)),
            pairs, pairs,
            pltpu.SemaphoreType.DMA((2 + 2 * others,)),
        ],
        compiler_params=pltpu.CompilerParams(
            collective_id=0, has_side_effects=True, vmem_limit_bytes=60 * 1024 * 1024),
    )(counts, tokens, cotangent, gate_w, up_w, down_w)


def shards(chips, tokens, cotangent, counts, w_gate, w_up, w_down):
    slots = tokens.shape[1]
    xs, acts, own, back, ret = call_rows(
        chips, counts, tokens[0], cotangent[0], w_gate[0], w_up[0], w_down[0])
    got = []
    for step in range(1, chips):
        pairs = [(q * 2 + c, (q - step) % chips * 2 + c) for q in range(chips) for c in range(2)]
        got.append(lax.ppermute(ret[step - 1], "dp", pairs))
    gate_grad = contract_first(xs[0], acts[1]).astype(jnp.bfloat16)
    up_grad = contract_first(xs[0], acts[2]).astype(jnp.bfloat16)
    down_grad = contract_first(acts[0], xs[1]).astype(jnp.bfloat16)
    firsts, seconds = own[0].astype(jnp.float32), own[1].astype(jnp.float32)
    for step in range(1, chips):
        firsts = firsts + got[step - 1].astype(jnp.float32)
        seconds = seconds + back[step - 1].astype(jnp.float32)
    sums = [
        jnp.concatenate([firsts[a], seconds[a, :slots - HALF]], axis=0).astype(jnp.bfloat16)
        for a in range(2)
    ]
    return (sums[0][None], sums[1][None], gate_grad[None], up_grad[None], down_grad[None])


def solution(mesh):
    by_row = P("expert", "dp", None)
    by_column = P("expert", None, "dp")
    return jax.shard_map(
        functools.partial(shards, mesh.shape["dp"] // 2),
        mesh=mesh,
        in_specs=(by_row, by_row, P(), by_column, by_column, by_row),
        out_specs=(by_row, by_row, by_column, by_column, by_row),
        check_vma=False,
    )
```
